128 devices in a mesh: frame: 8 (over z_lo, y), pixel: 16 (over x, z_hi, core).
Axes of the slice: x: 4, y: 4, z: 4 (z_hi: 2, z_lo: 2; z = z_hi * 2 + z_lo), core: 2. Of those that a mesh axis runs over, the one named last changes fastest.
Arguments:
- intensity: float32 [4096, 16384], P('frame', 'pixel'), may hold values from 0.2 to 180, as said below
- cycle_label: int32 [16384], P('pixel'), may hold values from 0 to 15, as said below
Outputs:
- correlation: float32 [16, 4096, 4096], P('pixel', 'frame')
The draws below stay inside these ranges and needn't reach their ends.
Inputs may be any that keep to these rules, and one draw needn't show every extreme that they name: `cycle_label`: labels never fall along the pixels; for r >= 1 the first pixel of cycle r lies before position r * 1024 and at most 512 positions before it; every cycle holds at least one pixel. `intensity`: positive intensities.
All inputs are finite; a program needn't handle non-finite values.
Results may differ from the reference program's by a relative error of at most 0.0003.
Values sent between devices are 32-bit elements; how exact they have to be, the bound alone decides.
A program may use at most 128 MiB of HBM per device.

```python
import jax
import jax.numpy as jnp
from jax import lax

CYCLES = 16
FRAMES = 4096
PIXELS = 16384


def draw_intensity(key, part):
    key = jax.random.fold_in(key, 11)
    key_frame = jax.random.fold_in(key, 1)
    key_pixel = jax.random.fold_in(key, 2)
    key_speckle = jax.random.fold_in(key, 3)
    frame_scale = jnp.exp(jax.random.uniform(key_frame, (FRAMES, 1), jnp.float32) * jnp.log(10.0))
    pixel_scale = jnp.exp(jax.random.uniform(key_pixel, (1, PIXELS), jnp.float32) * jnp.log(10.0))
    speckle = jax.random.uniform(key_speckle, (FRAMES, PIXELS), jnp.float32, 0.2, 1.8)
    return (frame_scale * pixel_scale * speckle).astype(jnp.float32)


def draw_cycle_label(key, part):
    key = jax.random.fold_in(key, 29)
    key_size = jax.random.fold_in(key, 1)
    mean_cycle = PIXELS // CYCLES
    bounds = jnp.arange(CYCLES + 1, dtype=jnp.int32)
    magnitude = jax.random.randint(key_size, (CYCLES + 1,), mean_cycle // 5, 2 * mean_cycle // 5 + 1, dtype=jnp.int32)
    wiggle = -magnitude
    wiggle = jnp.where(bounds == 2, -(mean_cycle // 2), wiggle)
    wiggle = jnp.where((bounds == 0) | (bounds == CYCLES), 0, wiggle)
    cuts = bounds * mean_cycle + wiggle
    positions = jnp.arange(PIXELS, dtype=jnp.int32)
    inner_cuts = cuts[1:CYCLES]
    return jnp.sum((positions[:, None] >= inner_cuts[None, :]).astype(jnp.int32), axis=1).astype(jnp.int32)


def setup_inputs(seed: int = 0) -> dict:
    key_of = jax.random.split(jax.random.key(seed), 3)
    return {
        "intensity": draw_intensity(jax.random.fold_in(key_of[2], 71), 0),
        "cycle_label": draw_cycle_label(jax.random.fold_in(key_of[2], 71), 0),
    }


def reference(intensity, cycle_label):
    cycle_ids = jnp.arange(CYCLES, dtype=jnp.int32)
    onehot_cycle = (cycle_label[:, None] == cycle_ids[None, :]).astype(intensity.dtype)
    cycle_sums = jnp.dot(intensity, onehot_cycle, precision=lax.Precision.HIGHEST)
    counts = jnp.sum(onehot_cycle, axis=0)
    block_size = 128
    blocks = PIXELS // block_size
    block_data = intensity.reshape(FRAMES, blocks, block_size).transpose(1, 0, 2)
    block_labels = cycle_label.reshape(blocks, block_size)

    def add_block(gram, pair):
        data, labels = pair
        first_cycle = labels[0]
        last_cycle = labels[block_size - 1]

        def add_cycle(cycle_id, gram_now):
            masked = data * (labels == cycle_id).astype(data.dtype)[None, :]
            product = lax.dot_general(masked, data, (((1,), (1,)), ((), ())), precision=lax.Precision.HIGHEST)
            return gram_now.at[cycle_id].add(product)

        return lax.fori_loop(first_cycle, last_cycle + 1, add_cycle, gram), None

    gram0 = jnp.zeros((CYCLES, FRAMES, FRAMES), intensity.dtype)
    gram, _ = lax.scan(add_block, gram0, (block_data, block_labels))
    sums_t = cycle_sums.T
    return gram * counts[:, None, None] / (sums_t[:, :, None] * sums_t[:, None, :])
```

```python
import functools

import jax
import jax.numpy as jnp
from jax import lax
from jax.experimental import pallas as pl
from jax.experimental.pallas import tpu as pltpu
from jax.sharding import PartitionSpec as P

MESH = pl.DeviceIdType.MESH

OWN, LOW, HIGH, FAR, PAIR = range(5)
ROWS, COLS, TAIL = 512, 1024, 512
HALF = ROWS // 2
TILE = 256
DEPTH = COLS + TAIL

NT = (((1,), (1,)), ((), ()))


def kernel(
    x_ref, label_ref, out_ref,
    xm, xt, tail_label, hi, lo, row_scale, col_scale, block,
    send, recv, local,
):
    f = lax.axis_index("frame")
    r = lax.axis_index("pixel")
    a, b = f // 4, f % 4
    f_high = a * 4 + (b + 1) % 4
    f_low = a * 4 + (b + 3) % 4
    f_far = a * 4 + (b + 2) % 4
    f_pair = (1 - a) * 4 + b
    even = r % 2 == 0
    odd = r % 2 == 1
    has_next = jnp.logical_and(odd, r < 15)
    has_prev = jnp.logical_and(even, r > 0)
    high, low, pair = (f_high, r), (f_low, r), (f_pair, r)
    twin = (f, r + 1 - 2 * (r % 2))
    following = (f_pair, r + 1)
    preceding = (f_pair, r - 1)

    barrier = pltpu.get_barrier_semaphore()
    for peer in (high, low, pair, twin):
        pl.semaphore_signal(barrier, inc=1, device_id=peer, device_id_type=MESH)

    @pl.when(has_next)
    def _():
        pl.semaphore_signal(barrier, inc=1, device_id=following, device_id_type=MESH)

    @pl.when(has_prev)
    def _():
        pl.semaphore_signal(barrier, inc=1, device_id=preceding, device_id_type=MESH)

    crossing = jnp.logical_or(has_next, has_prev)

    @pl.when(crossing)
    def _():
        pl.semaphore_wait(barrier, 5)

    @pl.when(jnp.logical_not(crossing))
    def _():
        pl.semaphore_wait(barrier, 4)

    names = {}

    def remote(name, src, dst, peer):
        i = names.setdefault(name, len(names))
        return pltpu.make_async_remote_copy(src, dst, send.at[i], recv.at[i], device_id=peer, device_id_type=MESH)

    part = [pl.ds(0, HALF), pl.ds(HALF, HALF)]
    tail_cols = pl.ds(COLS - TAIL, TAIL)

    up = [remote(f"up{h}", x_ref.at[part[h]], xm.at[LOW, part[h]], high) for h in range(2)]
    down = [remote(f"down{h}", x_ref.at[part[h]], xm.at[HIGH, part[h]], low) for h in range(2)]
    across = [remote(f"across{h}", x_ref.at[part[h]], xm.at[PAIR, part[h]], pair) for h in range(2)]
    tail_out = remote("tail_out", x_ref.at[:, tail_cols], xt.at[PAIR], following)
    label_out = remote("label_out", label_ref.at[:, tail_cols], tail_label, following)
    label_twin = remote("label_twin", label_ref.at[:, tail_cols], tail_label, twin)
    tail_pair = remote("tail_pair", xt.at[PAIR], xt.at[OWN], pair)
    tail_up = remote("tail_up", xt.at[OWN], xt.at[LOW], high)
    tail_down = remote("tail_down", xt.at[OWN], xt.at[HIGH], low)
    on_up = remote("on_up", xm.at[LOW, part[0]], xm.at[FAR, part[0]], high)
    on_down = remote("on_down", xm.at[HIGH, part[1]], xm.at[FAR, part[1]], low)
    tail_on_up = remote("tail_on_up", xt.at[LOW, part[0]], xt.at[FAR, part[0]], high)
    tail_on_down = remote("tail_on_down", xt.at[HIGH, part[1]], xt.at[FAR, part[1]], low)
    twin_own = remote("twin_own", x_ref.at[:, tail_cols], xt.at[OWN], twin)
    twin_slot = {s: remote(f"twin{s}", xm.at[s, :, tail_cols], xt.at[s], twin) for s in (LOW, HIGH, PAIR)}
    twin_far = [remote(f"twin_far{h}", xm.at[FAR, part[h], tail_cols], xt.at[FAR, part[h]], twin) for h in range(2)]

    def on(cond, *acts):
        @pl.when(cond)
        def _():
            for act in acts:
                act()

    own_copy = pltpu.make_async_copy(x_ref, xm.at[OWN], local.at[0])
    on(has_next, tail_out.start, label_out.start)
    on(even, twin_own.start, label_twin.start)
    for h in range(2):
        across[h].start()
    up[0].start()
    down[1].start()
    up[1].start()
    down[0].start()
    own_copy.start()

    @pl.when(has_prev)
    def _():
        label_out.wait_recv()
        tail_out.wait_recv()
        tail_pair.start()

    @pl.when(r == 0)
    def _():
        xt[OWN] = jnp.zeros((ROWS, TAIL), jnp.float32)
        xt[PAIR] = jnp.zeros((ROWS, TAIL), jnp.float32)
        tail_label[...] = jnp.full((1, TAIL), -1, jnp.int32)

    on(has_prev, tail_pair.wait_recv)
    on(even, tail_up.start, tail_down.start)
    on(odd, twin_own.wait_recv, label_twin.wait_recv)

    keep_main = label_ref[...] == r
    keep_tail = tail_label[...] == r
    counts = jnp.sum(keep_main.astype(jnp.float32)) + jnp.sum(keep_tail.astype(jnp.float32))

    def split(slot, start=0, rows=ROWS):
        step = 64

        def body(i, _):
            at = pl.ds(pl.multiple_of(start + i * step, step), step)
            total = jnp.zeros((step, 1), jnp.float32)
            for ref, keep, base, width in ((xt, keep_tail, 0, TAIL), (xm, keep_main, TAIL, COLS)):
                v = jnp.where(keep, ref[slot, at, :], 0.0)
                v_hi = v.astype(jnp.bfloat16)
                v_lo = (v - v_hi.astype(jnp.float32)).astype(jnp.bfloat16)
                hi[slot, at, base : base + width] = v_hi
                lo[slot, at, base : base + width] = v_lo
                total = total + jnp.sum(v, axis=1, keepdims=True)
            row_scale[slot, at, :] = counts / total
            return 0

        lax.fori_loop(0, rows // step, body, 0)
        ones = jnp.ones((8, DEPTH), jnp.bfloat16)
        at = pl.ds(start, rows)
        sums = lax.dot_general(ones, hi[slot, at, :], NT, preferred_element_type=jnp.float32)
        sums += lax.dot_general(ones, lo[slot, at, :], NT, preferred_element_type=jnp.float32)
        col_scale[slot, :, at] = 1.0 / sums

    def product(row_slot, col_slot, start, cols, place):
        def body(i, _):
            at = pl.ds(pl.multiple_of(start + i * TILE, TILE), TILE)
            l_hi, l_lo = hi[row_slot], lo[row_slot]
            r_hi, r_lo = hi[col_slot, at, :], lo[col_slot, at, :]
            dot = functools.partial(lax.dot_general, dimension_numbers=NT, preferred_element_type=jnp.float32)
            total = dot(l_hi, r_hi) + (dot(l_hi, r_lo) + dot(l_lo, r_hi))
            block[place, :, at] = total * row_scale[row_slot] * col_scale[col_slot, 0:1, at]
            return 0

        lax.fori_loop(0, cols // TILE, body, 0)

    pending = []

    def keep_block(place, owner, sem):
        copy = pltpu.make_async_copy(block.at[place], out_ref.at[0, :, pl.ds(pl.multiple_of(owner * ROWS, ROWS), ROWS)], local.at[sem])
        copy.start()
        pending.append(copy)

    def give(name, place, start, cols, owner, peer):
        dst = out_ref.at[0, :, pl.ds(pl.multiple_of(owner * ROWS + start, TILE), cols)]
        copy = remote(name, block.at[place, :, pl.ds(start, cols)], dst, peer)
        copy.start()
        return copy

    own_copy.wait()
    split(OWN)
    product(OWN, OWN, 0, ROWS, 0)
    keep_block(0, f, 1)

    up[0].wait_recv()
    on_up.start()
    down[1].wait_recv()
    on_down.start()
    up[1].wait_recv()
    down[0].wait_recv()
    on(even, twin_slot[LOW].start, twin_slot[HIGH].start)
    @pl.when(even)
    def _():
        tail_up.wait_recv()
        tail_on_up.start()
        tail_down.wait_recv()
        tail_on_down.start()

    for h in range(2):
        across[h].wait_recv()
    on(even, twin_slot[PAIR].start)
    on(odd, twin_slot[LOW].wait_recv, twin_slot[HIGH].wait_recv, twin_slot[PAIR].wait_recv)
    split(PAIR)
    split(LOW)
    product(PAIR, LOW, 0, HALF, 5)
    gifts = [give("pair_low", 5, 0, HALF, f_low, pair)]
    split(HIGH)
    product(PAIR, HIGH, 0, HALF, 6)
    gifts.append(give("pair_high", 6, 0, HALF, f_high, pair))

    product(OWN, PAIR, 0, ROWS, 4)
    keep_block(4, f_pair, 2)
    product(OWN, LOW, 0, ROWS, 1)
    keep_block(1, f_low, 3)
    product(OWN, HIGH, 0, ROWS, 2)
    keep_block(2, f_high, 4)

    product(LOW, PAIR, HALF, HALF, 5)
    gifts.append(give("low_pair", 5, HALF, HALF, f_pair, low))
    product(HIGH, PAIR, HALF, HALF, 6)
    gifts.append(give("high_pair", 6, HALF, HALF, f_pair, high))

    for h, main, tail in ((0, on_up, tail_on_up), (1, on_down, tail_on_down)):
        main.wait_recv()
        on(even, twin_far[h].start, tail.wait_recv)
        on(odd, twin_far[h].wait_recv)
        split(FAR, h * HALF, HALF)
        product(PAIR, FAR, h * HALF, HALF, 7)
        gifts.append(give(f"pair_far{h}", 7, h * HALF, HALF, f_far, pair))
    product(OWN, FAR, 0, ROWS, 3)
    keep_block(3, f_far, 5)

    for copy in up + down + across + [on_up, on_down]:
        copy.wait_send()
    on(has_next, tail_out.wait_send, label_out.wait_send)
    on(has_prev, tail_pair.wait_send)
    on(
        even,
        *(c.wait_send for c in [tail_up, tail_down, tail_on_up, tail_on_down, twin_own, label_twin]),
        *(c.wait_send for c in [*twin_slot.values(), *twin_far]),
    )
    for copy in gifts:
        copy.wait()
    for copy in pending:
        copy.wait()
    assert len(names) <= SEMAPHORES


SEMAPHORES = 32


def shards(intensity, cycle_label):
    rows, cols = intensity.shape
    return pl.pallas_call(
        kernel,
        out_shape=jax.ShapeDtypeStruct((1, ROWS, 8 * ROWS), jnp.float32),
        in_specs=[pl.BlockSpec(memory_space=pl.ANY), pl.BlockSpec(memory_space=pltpu.VMEM)],
        out_specs=pl.BlockSpec(memory_space=pl.ANY),
        scratch_shapes=[
            pltpu.VMEM((5, ROWS, COLS), jnp.float32),
            pltpu.VMEM((5, ROWS, TAIL), jnp.float32),
            pltpu.VMEM((1, TAIL), jnp.int32),
            pltpu.VMEM((5, ROWS, DEPTH), jnp.bfloat16),
            pltpu.VMEM((5, ROWS, DEPTH), jnp.bfloat16),
            pltpu.VMEM((5, ROWS, 1), jnp.float32),
            pltpu.VMEM((5, 8, ROWS), jnp.float32),
            pltpu.VMEM((8, ROWS, ROWS), jnp.float32),
            pltpu.SemaphoreType.DMA((SEMAPHORES,)),
            pltpu.SemaphoreType.DMA((SEMAPHORES,)),
            pltpu.SemaphoreType.DMA((8,)),
        ],
        compiler_params=pltpu.CompilerParams(collective_id=0, has_side_effects=True, vmem_limit_bytes=56 << 20),
        name="gram_maps",
    )(intensity, cycle_label.reshape(1, cols))


def solution(mesh):
    in_specs = (P("frame", "pixel"), P("pixel"))
    out_specs = P("pixel", "frame", None)
    return jax.shard_map(shards, mesh=mesh, in_specs=in_specs, out_specs=out_specs, check_vma=False)
```

```python
import functools

import jax
import jax.numpy as jnp
from jax import lax
from jax.experimental import pallas as pl
from jax.experimental.pallas import tpu as pltpu
from jax.sharding import PartitionSpec as P

MESH = pl.DeviceIdType.MESH

OWN, LOW, HIGH, FAR, PAIR = range(5)
ROWS, COLS, TAIL = 512, 1024, 512
HALF = ROWS // 2
CHUNK = ROWS // 4
TILE = 256
DEPTH = COLS + TAIL

NT = (((1,), (1,)), ((), ()))


def kernel(
    x_ref, label_hbm, out_ref,
    xm, xt, label_ref, tail_label, hi, lo, row_scale, col_scale, inverse, block,
    send, recv, local,
):
    f = lax.axis_index("frame")
    r = lax.axis_index("pixel")
    a, b = f // 4, f % 4
    f_high = a * 4 + (b + 1) % 4
    f_low = a * 4 + (b + 3) % 4
    f_far = a * 4 + (b + 2) % 4
    f_pair = (1 - a) * 4 + b
    even = r % 2 == 0
    odd = r % 2 == 1
    has_next = jnp.logical_and(odd, r < 15)
    has_prev = jnp.logical_and(even, r > 0)
    high, low, pair = (f_high, r), (f_low, r), (f_pair, r)
    twin = (f, r + 1 - 2 * (r % 2))
    following = (f_pair, r + 1)
    preceding = (f_pair, r - 1)

    barrier = pltpu.get_barrier_semaphore()
    for peer in (high, low, pair, twin):
        pl.semaphore_signal(barrier, inc=1, device_id=peer, device_id_type=MESH)

    @pl.when(has_next)
    def _():
        pl.semaphore_signal(barrier, inc=1, device_id=following, device_id_type=MESH)

    @pl.when(has_prev)
    def _():
        pl.semaphore_signal(barrier, inc=1, device_id=preceding, device_id_type=MESH)

    crossing = jnp.logical_or(has_next, has_prev)

    @pl.when(crossing)
    def _():
        pl.semaphore_wait(barrier, 5)

    @pl.when(jnp.logical_not(crossing))
    def _():
        pl.semaphore_wait(barrier, 4)

    names = {}

    def remote(name, src, dst, peer):
        i = names.setdefault(name, len(names))
        return pltpu.make_async_remote_copy(src, dst, send.at[i], recv.at[i], device_id=peer, device_id_type=MESH)

    part = [pl.ds(0, HALF), pl.ds(HALF, HALF)]
    chunk = [pl.ds(i * CHUNK, CHUNK) for i in range(ROWS // CHUNK)]
    tail_cols = pl.ds(COLS - TAIL, TAIL)
    head_cols = pl.ds(0, COLS - TAIL)

    up = [remote(f"up{h}", x_ref.at[part[h]], xm.at[LOW, part[h]], high) for h in range(2)]
    down = [remote(f"down{h}", x_ref.at[part[h]], xm.at[HIGH, part[h]], low) for h in range(2)]
    across = [
        remote(f"across{h}", x_ref.at[part[h], tail_cols], xm.at[PAIR, part[h], tail_cols], pair) for h in range(2)
    ] + [remote("across2", x_ref.at[:, head_cols], xm.at[PAIR, :, head_cols], pair)]
    tail_out = remote("tail_out", x_ref.at[:, tail_cols], xt.at[PAIR], following)
    relay = [
        remote(f"relay{h}", xm.at[PAIR, part[h], tail_cols], xt.at[OWN, part[h]], following) for h in range(2)
    ]
    label_out = remote("label_out", label_hbm.at[:, tail_cols], tail_label, following)
    label_twin = remote("label_twin", label_hbm.at[:, tail_cols], tail_label, twin)
    tail_up = remote("tail_up", xt.at[OWN], xt.at[LOW], high)
    tail_down = remote("tail_down", xt.at[OWN], xt.at[HIGH], low)
    far_from = [(LOW, high), (LOW, high), (HIGH, low), (HIGH, low)]
    far = [
        remote(f"far{i}", xm.at[slot, chunk[i]], xm.at[FAR, chunk[i]], peer) for i, (slot, peer) in enumerate(far_from)
    ]
    tail_far = [
        remote(f"tail_far{i}", xt.at[slot, chunk[i]], xt.at[FAR, chunk[i]], peer)
        for i, (slot, peer) in enumerate(far_from)
    ]
    twin_own = remote("twin_own", x_ref.at[:, tail_cols], xt.at[OWN], twin)
    twin_slot = {s: remote(f"twin{s}", xm.at[s, :, tail_cols], xt.at[s], twin) for s in (LOW, HIGH, PAIR)}
    twin_far = [remote(f"twin_far{i}", xm.at[FAR, chunk[i], tail_cols], xt.at[FAR, chunk[i]], twin) for i in range(4)]

    def on(cond, *acts):
        @pl.when(cond)
        def _():
            for act in acts:
                act()

    own_copy = pltpu.make_async_copy(x_ref, xm.at[OWN], local.at[0])
    label_copy = pltpu.make_async_copy(label_hbm, label_ref, local.at[1])
    label_copy.start()
    on(has_next, tail_out.start, label_out.start)
    on(even, twin_own.start, label_twin.start)
    for h in range(3):
        across[h].start()
    up[0].start()
    down[1].start()
    up[1].start()
    down[0].start()
    own_copy.start()

    @pl.when(has_prev)
    def _():
        label_out.wait_recv()

    on(odd, label_twin.wait_recv)
    label_copy.wait()

    @pl.when(r == 0)
    def _():
        xt[OWN] = jnp.zeros((ROWS, TAIL), jnp.float32)
        xt[PAIR] = jnp.zeros((ROWS, TAIL), jnp.float32)
        tail_label[...] = jnp.full((1, TAIL), -1, jnp.int32)

    keep_main = label_ref[...] == r
    keep_tail = tail_label[...] == r
    counts = jnp.sum(keep_main.astype(jnp.float32)) + jnp.sum(keep_tail.astype(jnp.float32))

    def split(slot, start=0, rows=ROWS, place=None):
        step = 64
        place = start if place is None else place

        def body(i, _):
            at = pl.ds(pl.multiple_of(start + i * step, step), step)
            to = pl.ds(pl.multiple_of(place + i * step, step), step)
            total = jnp.zeros((step, 1), jnp.float32)
            for ref, keep, base, width in ((xt, keep_tail, 0, TAIL), (xm, keep_main, TAIL, COLS)):
                v = jnp.where(keep, ref[slot, at, :], 0.0)
                v_hi = v.astype(jnp.bfloat16)
                v_lo = (v - v_hi.astype(jnp.float32)).astype(jnp.bfloat16)
                hi[slot, to, base : base + width] = v_hi
                lo[slot, to, base : base + width] = v_lo
                total = total + jnp.sum(v, axis=1, keepdims=True)
            row_scale[slot, to, :] = counts / total
            inverse[to, :] = jnp.broadcast_to(1.0 / total, (step, 128))
            return 0

        lax.fori_loop(0, rows // step, body, 0)
        for i in range(rows // 128):
            to = pl.ds(place + i * 128, 128)
            col_scale[slot, :, to] = inverse[to, :].T[0:8, :]

    def product(row_slot, col_slot, start, cols, place, place_start):
        tile = min(cols, TILE)

        def body(i, _):
            at = pl.ds(pl.multiple_of(start + i * tile, tile), tile)
            to = pl.ds(pl.multiple_of(place_start + i * tile, tile), tile)
            l_hi, l_lo = hi[row_slot], lo[row_slot]
            r_hi, r_lo = hi[col_slot, at, :], lo[col_slot, at, :]
            dot = functools.partial(lax.dot_general, dimension_numbers=NT, preferred_element_type=jnp.float32)
            total = dot(l_hi, r_hi) + (dot(l_hi, r_lo) + dot(l_lo, r_hi))
            total = total * row_scale[row_slot] * col_scale[col_slot, 0:1, at]
            if col_slot == FAR:
                for half in range(2):
                    to = pl.ds(pl.multiple_of(place_start + half * HALF + i * CHUNK, CHUNK), CHUNK)
                    place[:, to] = total[:, half * CHUNK : (half + 1) * CHUNK]
            else:
                place[:, to] = total
            return 0

        lax.fori_loop(0, cols // tile, body, 0)

    def keep(slot, owner):
        product(OWN, slot, 0, ROWS, out_ref.at[0], owner * ROWS)

    gifts = []

    def hand(place, start, cols, owner, peer):
        dst = out_ref.at[0, :, pl.ds(pl.multiple_of(owner * ROWS + start, CHUNK), cols)]
        copy = remote(f"gift{len(gifts)}", block.at[place, :, pl.ds(start, cols)], dst, peer)
        gifts.append(copy)
        return copy

    def make(row_slot, col_slot, start, cols, place, owner, peer):
        product(row_slot, col_slot, start, cols, block.at[place], start)
        return hand(place, start, cols, owner, peer)

    own_copy.wait()
    on(odd, twin_own.wait_recv)

    @pl.when(has_prev)
    def _():
        tail_out.wait_recv()
        for h in range(2):
            relay[h].wait_recv()

    on(even, tail_up.start, tail_down.start)
    split(OWN)
    keep(OWN, f)

    for h in range(2):
        across[h].wait_recv()

        @pl.when(has_next)
        def _(h=h):
            relay[h].start()

    for h in range(2):
        up[h].wait_recv()
    on(even, twin_slot[LOW].start)
    across[2].wait_recv()
    on(even, twin_slot[PAIR].start)
    for h in range(2):
        down[h].wait_recv()
    on(even, twin_slot[HIGH].start)

    @pl.when(even)
    def _():
        far[0].start()
        far[2].start()

    on(odd, twin_slot[PAIR].wait_recv)
    split(PAIR)

    @pl.when(even)
    def _():
        tail_up.wait_recv()
        tail_far[0].start()
        far[1].start()
        tail_far[1].start()
        tail_down.wait_recv()
        tail_far[2].start()
        far[3].start()
        tail_far[3].start()

    on(odd, twin_slot[LOW].wait_recv)
    split(LOW)
    make(PAIR, LOW, 0, HALF, 0, f_low, pair).start()
    on(odd, twin_slot[HIGH].wait_recv)
    split(HIGH)
    make(PAIR, HIGH, 0, HALF, 1, f_high, pair).start()

    @pl.when(odd)
    def _():
        for i in (0, 2, 1, 3):
            far[i].start()

    below = make(LOW, PAIR, HALF, HALF, 0, f_pair, low)
    above = make(HIGH, PAIR, HALF, HALF, 1, f_pair, high)
    on(even, below.start, above.start)
    keep(PAIR, f_pair)
    keep(LOW, f_low)
    keep(HIGH, f_high)

    for n in range(2):
        for half in range(2):
            i = n + 2 * half
            far[i].wait_recv()
            on(even, twin_far[i].start, tail_far[i].wait_recv)
            on(odd, twin_far[i].wait_recv)
            split(FAR, i * CHUNK, CHUNK, n * HALF + half * CHUNK)
        if n == 1:
            on(odd, below.start, above.start)
        product(PAIR, FAR, n * HALF, HALF, block.at[2], n * CHUNK)
        for half in range(2):
            hand(2, half * HALF + n * CHUNK, CHUNK, f_far, pair).start()
    keep(FAR, f_far)

    for copy in up + down + across + far:
        copy.wait_send()
    on(has_next, tail_out.wait_send, label_out.wait_send, relay[0].wait_send, relay[1].wait_send)
    on(
        even,
        *(c.wait_send for c in [tail_up, tail_down, twin_own, label_twin]),
        *(c.wait_send for c in [*tail_far, *twin_slot.values(), *twin_far]),
    )
    for copy in gifts:
        copy.wait()
    assert len(names) <= SEMAPHORES


SEMAPHORES = 48


def shards(intensity, cycle_label):
    rows, cols = intensity.shape
    return pl.pallas_call(
        kernel,
        out_shape=pltpu.VMEM((1, ROWS, 8 * ROWS), jnp.float32),
        in_specs=[pl.BlockSpec(memory_space=pltpu.HBM), pl.BlockSpec(memory_space=pltpu.HBM)],
        out_specs=pl.BlockSpec(memory_space=pltpu.VMEM),
        scratch_shapes=[
            pltpu.VMEM((5, ROWS, COLS), jnp.float32),
            pltpu.VMEM((5, ROWS, TAIL), jnp.float32),
            pltpu.VMEM((1, COLS), jnp.int32),
            pltpu.VMEM((1, TAIL), jnp.int32),
            pltpu.VMEM((5, ROWS, DEPTH), jnp.bfloat16),
            pltpu.VMEM((5, ROWS, DEPTH), jnp.bfloat16),
            pltpu.VMEM((5, ROWS, 1), jnp.float32),
            pltpu.VMEM((5, 8, ROWS), jnp.float32),
            pltpu.VMEM((ROWS, 128), jnp.float32),
            pltpu.VMEM((3, ROWS, ROWS), jnp.float32),
            pltpu.SemaphoreType.DMA((SEMAPHORES,)),
            pltpu.SemaphoreType.DMA((SEMAPHORES,)),
            pltpu.SemaphoreType.DMA((2,)),
        ],
        compiler_params=pltpu.CompilerParams(collective_id=0, has_side_effects=True, vmem_limit_bytes=55 << 20),
        name="gram_maps",
    )(intensity, cycle_label.reshape(1, cols))


def solution(mesh):
    in_specs = (P("frame", "pixel"), P("pixel"))
    out_specs = P("pixel", "frame", None)
    return jax.shard_map(shards, mesh=mesh, in_specs=in_specs, out_specs=out_specs, check_vma=False)
```

```python
import functools

import jax
import jax.numpy as jnp
from jax import lax
from jax.experimental import pallas as pl
from jax.experimental.pallas import tpu as pltpu
from jax.sharding import PartitionSpec as P

MESH = pl.DeviceIdType.MESH

OWN, NEXT, FAR, PAIR = range(4)
ROWS, COLS, TAIL = 512, 1024, 512
HALF = ROWS // 2
TILE = 256
DEPTH = COLS + TAIL

NT = (((1,), (1,)), ((), ()))


def kernel(
    x_ref, label_hbm, out_ref,
    xm, xt, label_ref, tail_label, hi, lo, row_scale, col_scale, inverse, block,
    send, recv, local, go,
):
    f = lax.axis_index("frame")
    r = lax.axis_index("pixel")
    a, b = f // 4, f % 4
    turn = 2 * (r % 2)
    f_next = a * 4 + (b + 1 + turn) % 4
    f_last = a * 4 + (b + 3 - turn) % 4
    f_far = a * 4 + (b + 2) % 4
    f_pair = (1 - a) * 4 + b
    even = r % 2 == 0
    odd = r % 2 == 1
    has_next = jnp.logical_and(odd, r < 15)
    has_prev = jnp.logical_and(even, r > 0)
    nxt, last, pair = (f_next, r), (f_last, r), (f_pair, r)
    twin = (f, r + 1 - turn)
    following = (f_pair, r + 1)
    preceding = (f_pair, r - 1)

    barrier = pltpu.get_barrier_semaphore()
    for peer in (nxt, last, pair, twin):
        pl.semaphore_signal(barrier, inc=1, device_id=peer, device_id_type=MESH)

    @pl.when(has_next)
    def _():
        pl.semaphore_signal(barrier, inc=1, device_id=following, device_id_type=MESH)

    @pl.when(has_prev)
    def _():
        pl.semaphore_signal(barrier, inc=1, device_id=preceding, device_id_type=MESH)

    crossing = jnp.logical_or(has_next, has_prev)

    @pl.when(crossing)
    def _():
        pl.semaphore_wait(barrier, 5)

    @pl.when(jnp.logical_not(crossing))
    def _():
        pl.semaphore_wait(barrier, 4)

    names = {}

    def remote(name, src, dst, peer):
        i = names.setdefault(name, len(names))
        return pltpu.make_async_remote_copy(src, dst, send.at[i], recv.at[i], device_id=peer, device_id_type=MESH)

    part = [pl.ds(0, HALF), pl.ds(HALF, HALF)]
    tail_cols = pl.ds(COLS - TAIL, TAIL)
    head_cols = pl.ds(0, COLS - TAIL)

    along = [remote(f"along{h}", x_ref.at[part[h]], xm.at[NEXT, part[h]], last) for h in range(2)]
    far = [remote(f"far{h}", xm.at[NEXT, part[h]], xm.at[FAR, part[h]], last) for h in range(2)]
    tail_along = remote("tail_along", xt.at[OWN], xt.at[NEXT], last)
    tail_far = [remote(f"tail_far{h}", xt.at[NEXT, part[h]], xt.at[FAR, part[h]], last) for h in range(2)]
    across = [
        remote(f"across{c}{h}", x_ref.at[part[h], cols], xm.at[PAIR, part[h], cols], pair)
        for c, cols in enumerate((tail_cols, head_cols))
        for h in range(2)
    ]
    tail_out = remote("tail_out", x_ref.at[:, tail_cols], xt.at[PAIR], following)
    relay = [
        remote(f"relay{h}", xm.at[PAIR, part[h], tail_cols], xt.at[OWN, part[h]], following) for h in range(2)
    ]
    label_out = remote("label_out", label_hbm.at[:, tail_cols], tail_label, following)
    label_twin = remote("label_twin", label_hbm.at[:, tail_cols], tail_label, twin)
    twin_own = remote("twin_own", x_ref.at[:, tail_cols], xt.at[OWN], twin)
    twin_pair, twin_far = (
        [remote(f"twin{s}{h}", xm.at[s, part[h], tail_cols], xt.at[s, part[h]], twin) for h in range(2)]
        for s in (PAIR, FAR)
    )

    def on(cond, *acts):
        @pl.when(cond)
        def _():
            for act in acts:
                act()

    own_copy = pltpu.make_async_copy(x_ref, xm.at[OWN], local.at[0])
    label_copy = pltpu.make_async_copy(label_hbm, label_ref, local.at[1])
    label_copy.start()
    on(has_next, tail_out.start, label_out.start)
    on(even, twin_own.start, label_twin.start)
    for h in range(4):
        across[h].start()
    for h in range(2):
        along[h].start()
    own_copy.start()

    @pl.when(has_prev)
    def _():
        label_out.wait_recv()

    on(odd, label_twin.wait_recv)
    label_copy.wait()

    @pl.when(r == 0)
    def _():
        xt[OWN] = jnp.zeros((ROWS, TAIL), jnp.float32)
        xt[PAIR] = jnp.zeros((ROWS, TAIL), jnp.float32)
        tail_label[...] = jnp.full((1, TAIL), -1, jnp.int32)

    keep_main = label_ref[...] == r
    keep_tail = tail_label[...] == r
    counts = jnp.sum(keep_main.astype(jnp.float32)) + jnp.sum(keep_tail.astype(jnp.float32))

    def split(slot, start=0, rows=ROWS, place=None):
        step = 64
        place = start if place is None else place

        def body(i, _):
            at = pl.ds(pl.multiple_of(start + i * step, step), step)
            to = pl.ds(pl.multiple_of(place + i * step, step), step)
            total = jnp.zeros((step, 1), jnp.float32)
            for ref, keep, base, width in ((xt, keep_tail, 0, TAIL), (xm, keep_main, TAIL, COLS)):
                v = jnp.where(keep, ref[slot, at, :], 0.0)
                v_hi = v.astype(jnp.bfloat16)
                v_lo = (v - v_hi.astype(jnp.float32)).astype(jnp.bfloat16)
                hi[slot, to, base : base + width] = v_hi
                lo[slot, to, base : base + width] = v_lo
                total = total + jnp.sum(v, axis=1, keepdims=True)
            row_scale[slot, to, :] = counts / total
            inverse[to, :] = jnp.broadcast_to(1.0 / total, (step, 128))
            return 0

        lax.fori_loop(0, rows // step, body, 0)
        for i in range(rows // 128):
            to = pl.ds(place + i * 128, 128)
            col_scale[slot, :, to] = inverse[to, :].T[0:8, :]

    def product(row_slot, col_slot, place, place_start, start=0, rows=ROWS):
        def body(i, _):
            at = pl.ds(pl.multiple_of(i * TILE, TILE), TILE)
            to = pl.ds(pl.multiple_of(place_start + i * TILE, TILE), TILE)
            up = pl.ds(start, rows)
            l_hi, l_lo = hi[row_slot, up, :], lo[row_slot, up, :]
            r_hi, r_lo = hi[col_slot, at, :], lo[col_slot, at, :]
            dot = functools.partial(lax.dot_general, dimension_numbers=NT, preferred_element_type=jnp.float32)
            total = dot(l_hi, r_hi) + (dot(l_hi, r_lo) + dot(l_lo, r_hi))
            place[up, to] = total * row_scale[row_slot, up, :] * col_scale[col_slot, 0:1, at]
            return 0

        lax.fori_loop(0, ROWS // TILE, body, 0)

    def keep(slot, owner):
        product(OWN, slot, out_ref.at[0], owner * ROWS)

    gifts = []

    def make(place, row_slot, col_slot, owner, peer, start=0, rows=ROWS):
        product(row_slot, col_slot, block.at[place], 0, start, rows)
        up = pl.ds(start, rows)
        dst = out_ref.at[0, up, pl.ds(pl.multiple_of(owner * ROWS, ROWS), ROWS)]
        copy = remote(f"gift{len(gifts)}", block.at[place, up], dst, peer)
        gifts.append(copy)
        return copy

    own_copy.wait()

    @pl.when(odd)
    def _():
        twin_own.wait_recv()
        tail_along.start()
        for h in range(2):
            across[h].wait_recv()

            @pl.when(has_next)
            def _(h=h):
                relay[h].start()

            along[h].wait_recv()
            far[h].start()

    @pl.when(even)
    def _():
        for h in range(2):
            across[h].wait_recv()
            twin_pair[h].start()
        along[0].wait_recv()
        far[0].start()

        @pl.when(has_prev)
        def _():
            tail_out.wait_recv()
            for h in range(2):
                relay[h].wait_recv()

        tail_along.start()
        along[1].wait_recv()
        far[1].start()

    split(OWN)
    keep(OWN, f)

    across[2].wait_recv()
    on(odd, twin_pair[0].wait_recv)
    split(PAIR, 0, HALF)
    tail_along.wait_recv()
    on(even, tail_far[0].start, tail_far[1].start)
    split(NEXT)
    make(0, PAIR, NEXT, f_next, pair, 0, HALF).start()
    across[3].wait_recv()
    on(odd, twin_pair[1].wait_recv)
    split(PAIR, HALF, HALF)
    make(0, PAIR, NEXT, f_next, pair, HALF, HALF).start()

    near = [make(2, NEXT, OWN, f, nxt)]
    on(even, near[0].start)
    near.append(make(3, NEXT, PAIR, f_pair, nxt))
    on(even, near[1].start)
    keep(PAIR, f_pair)

    for h in range(2):
        far[h].wait_recv()
        on(even, twin_far[h].start)
    keep(NEXT, f_next)
    for h in range(2):
        on(odd, twin_far[h].wait_recv)

        @pl.when(even)
        def _(h=h):
            tail_far[h].wait_recv()
            if h == GO_AT:
                pl.semaphore_signal(go, inc=1, device_id=twin, device_id_type=MESH)

        split(FAR, h * HALF, HALF)
    make(1, PAIR, FAR, f_far, pair).start()

    @pl.when(odd)
    def _():
        pl.semaphore_wait(go, 1)
        for copy in near:
            copy.start()

    keep(FAR, f_far)

    for copy in along + far + across + [tail_along]:
        copy.wait_send()
    on(has_next, tail_out.wait_send, label_out.wait_send, relay[0].wait_send, relay[1].wait_send)
    on(even, *(c.wait_send for c in [*tail_far, *twin_pair, *twin_far, twin_own, label_twin]))
    for copy in gifts:
        copy.wait()
    assert len(names) <= SEMAPHORES


SEMAPHORES = 32
GO_AT = 0


def shards(intensity, cycle_label):
    rows, cols = intensity.shape
    return pl.pallas_call(
        kernel,
        out_shape=pltpu.VMEM((1, ROWS, 8 * ROWS), jnp.float32),
        in_specs=[pl.BlockSpec(memory_space=pltpu.HBM), pl.BlockSpec(memory_space=pltpu.HBM)],
        out_specs=pl.BlockSpec(memory_space=pltpu.VMEM),
        scratch_shapes=[
            pltpu.VMEM((4, ROWS, COLS), jnp.float32),
            pltpu.VMEM((4, ROWS, TAIL), jnp.float32),
            pltpu.VMEM((1, COLS), jnp.int32),
            pltpu.VMEM((1, TAIL), jnp.int32),
            pltpu.VMEM((4, ROWS, DEPTH), jnp.bfloat16),
            pltpu.VMEM((4, ROWS, DEPTH), jnp.bfloat16),
            pltpu.VMEM((4, ROWS, 1), jnp.float32),
            pltpu.VMEM((4, 8, ROWS), jnp.float32),
            pltpu.VMEM((ROWS, 128), jnp.float32),
            pltpu.VMEM((4, ROWS, ROWS), jnp.float32),
            pltpu.SemaphoreType.DMA((SEMAPHORES,)),
            pltpu.SemaphoreType.DMA((SEMAPHORES,)),
            pltpu.SemaphoreType.DMA((2,)),
            pltpu.SemaphoreType.REGULAR,
        ],
        compiler_params=pltpu.CompilerParams(collective_id=0, has_side_effects=True, vmem_limit_bytes=55 << 20),
        name="gram_maps",
    )(intensity, cycle_label.reshape(1, cols))


def solution(mesh):
    in_specs = (P("frame", "pixel"), P("pixel"))
    out_specs = P("pixel", "frame", None)
    return jax.shard_map(shards, mesh=mesh, in_specs=in_specs, out_specs=out_specs, check_vma=False)
```

```python
import functools

import jax
import jax.numpy as jnp
from jax import lax
from jax.experimental import pallas as pl
from jax.experimental.pallas import tpu as pltpu
from jax.sharding import PartitionSpec as P

MESH = pl.DeviceIdType.MESH

OWN, NEXT, FAR, PAIR = range(4)
ROWS, COLS, TAIL = 512, 1024, 512
HALF = ROWS // 2
TILE = 256
DEPTH = COLS + TAIL

NT = (((1,), (1,)), ((), ()))


def kernel(
    x_ref, label_hbm, out_ref,
    xm, xt, passing, label_ref, tail_label, hi, lo, row_scale, col_scale, inverse, block,
    send, recv, local, go,
):
    f = lax.axis_index("frame")
    r = lax.axis_index("pixel")
    a, b = f // 4, f % 4
    turn = 2 * (r % 2)
    f_next = a * 4 + (b + 1 + turn) % 4
    f_last = a * 4 + (b + 3 - turn) % 4
    f_far = a * 4 + (b + 2) % 4
    f_pair = (1 - a) * 4 + b
    even = r % 2 == 0
    odd = r % 2 == 1
    has_next = jnp.logical_and(odd, r < 15)
    has_prev = jnp.logical_and(even, r > 0)
    nxt, last, pair = (f_next, r), (f_last, r), (f_pair, r)
    twin = (f, r + 1 - turn)
    following = (f_pair, r + 1)
    preceding = (f_pair, r - 1)

    barrier = pltpu.get_barrier_semaphore()
    for peer in (nxt, last, pair, twin):
        pl.semaphore_signal(barrier, inc=1, device_id=peer, device_id_type=MESH)

    @pl.when(has_next)
    def _():
        pl.semaphore_signal(barrier, inc=1, device_id=following, device_id_type=MESH)

    @pl.when(has_prev)
    def _():
        pl.semaphore_signal(barrier, inc=1, device_id=preceding, device_id_type=MESH)

    crossing = jnp.logical_or(has_next, has_prev)

    @pl.when(crossing)
    def _():
        pl.semaphore_wait(barrier, 5)

    @pl.when(jnp.logical_not(crossing))
    def _():
        pl.semaphore_wait(barrier, 4)

    names = {}

    def remote(name, src, dst, peer):
        i = names.setdefault(name, len(names))
        return pltpu.make_async_remote_copy(src, dst, send.at[i], recv.at[i], device_id=peer, device_id_type=MESH)

    part = [pl.ds(0, HALF), pl.ds(HALF, HALF)]
    around = pl.ds(0, AROUND)
    rest = [pl.ds(AROUND, HALF - AROUND), pl.ds(HALF, HALF)]
    tail_cols = pl.ds(COLS - TAIL, TAIL)
    head_cols = pl.ds(0, COLS - TAIL)

    along = [remote(f"along{h}", x_ref.at[part[h]], xm.at[NEXT, part[h]], last) for h in range(2)]
    far = [remote(f"far{h}", xm.at[NEXT, part[h]], xm.at[FAR, part[h]], last) for h in range(2)]
    tail_along = remote("tail_along", xt.at[OWN], xt.at[NEXT], last)
    tail_far = [remote(f"tail_far{h}", xt.at[NEXT, p], xt.at[FAR, p], last) for h, p in enumerate(rest)]
    round_one = remote("round_one", xt.at[OWN, around], passing, nxt)
    round_two = remote("round_two", passing, xt.at[FAR, around], nxt)
    across = [
        remote(f"across{c}{h}", x_ref.at[part[h], cols], xm.at[PAIR, part[h], cols], pair)
        for c, cols in enumerate((tail_cols, head_cols))
        for h in range(2)
    ]
    tail_out = remote("tail_out", x_ref.at[:, tail_cols], xt.at[PAIR], following)
    relay = [
        remote(f"relay{h}", xm.at[PAIR, part[h], tail_cols], xt.at[OWN, part[h]], following) for h in range(2)
    ]
    label_out = remote("label_out", label_hbm.at[:, tail_cols], tail_label, following)
    label_twin = remote("label_twin", label_hbm.at[:, tail_cols], tail_label, twin)
    twin_own = remote("twin_own", x_ref.at[:, tail_cols], xt.at[OWN], twin)
    twin_pair, twin_far = (
        [remote(f"twin{s}{h}", xm.at[s, part[h], tail_cols], xt.at[s, part[h]], twin) for h in range(2)]
        for s in (PAIR, FAR)
    )

    def on(cond, *acts):
        @pl.when(cond)
        def _():
            for act in acts:
                act()

    own_copy = pltpu.make_async_copy(x_ref, xm.at[OWN], local.at[0])
    label_copy = pltpu.make_async_copy(label_hbm, label_ref, local.at[1])
    label_copy.start()
    on(has_next, tail_out.start, label_out.start)
    on(even, twin_own.start, label_twin.start)
    for h in range(4):
        across[h].start()
    for h in range(2):
        along[h].start()
    own_copy.start()

    @pl.when(has_prev)
    def _():
        label_out.wait_recv()

    on(odd, label_twin.wait_recv)
    label_copy.wait()

    @pl.when(r == 0)
    def _():
        xt[OWN] = jnp.zeros((ROWS, TAIL), jnp.float32)
        xt[PAIR] = jnp.zeros((ROWS, TAIL), jnp.float32)
        tail_label[...] = jnp.full((1, TAIL), -1, jnp.int32)

    keep_main = label_ref[...] == r
    keep_tail = tail_label[...] == r
    counts = jnp.sum(keep_main.astype(jnp.float32)) + jnp.sum(keep_tail.astype(jnp.float32))

    def split(slot, start=0, rows=ROWS, place=None):
        step = 64
        place = start if place is None else place

        def body(i, _):
            at = pl.ds(pl.multiple_of(start + i * step, step), step)
            to = pl.ds(pl.multiple_of(place + i * step, step), step)
            total = jnp.zeros((step, 1), jnp.float32)
            for ref, keep, base, width in ((xt, keep_tail, 0, TAIL), (xm, keep_main, TAIL, COLS)):
                v = jnp.where(keep, ref[slot, at, :], 0.0)
                v_hi = v.astype(jnp.bfloat16)
                v_lo = (v - v_hi.astype(jnp.float32)).astype(jnp.bfloat16)
                hi[slot, to, base : base + width] = v_hi
                lo[slot, to, base : base + width] = v_lo
                total = total + jnp.sum(v, axis=1, keepdims=True)
            row_scale[slot, to, :] = counts / total
            inverse[to, :] = jnp.broadcast_to(1.0 / total, (step, 128))
            return 0

        lax.fori_loop(0, rows // step, body, 0)
        for i in range(rows // 128):
            to = pl.ds(place + i * 128, 128)
            col_scale[slot, :, to] = inverse[to, :].T[0:8, :]

    def product(row_slot, col_slot, place, place_start, start=0, rows=ROWS, col=0, cols=ROWS):
        def body(i, _):
            at = pl.ds(pl.multiple_of(col + i * TILE, TILE), TILE)
            to = pl.ds(pl.multiple_of(place_start + col + i * TILE, TILE), TILE)
            up = pl.ds(start, rows)
            l_hi, l_lo = hi[row_slot, up, :], lo[row_slot, up, :]
            r_hi, r_lo = hi[col_slot, at, :], lo[col_slot, at, :]
            dot = functools.partial(lax.dot_general, dimension_numbers=NT, preferred_element_type=jnp.float32)
            total = dot(l_hi, r_hi) + (dot(l_hi, r_lo) + dot(l_lo, r_hi))
            place[up, to] = total * row_scale[row_slot, up, :] * col_scale[col_slot, 0:1, at]
            return 0

        lax.fori_loop(0, cols // TILE, body, 0)

    def keep(slot, owner):
        product(OWN, slot, out_ref.at[0], owner * ROWS)

    gifts = []

    def make(place, row_slot, col_slot, owner, peer, start=0, rows=ROWS, col=0, cols=ROWS):
        product(row_slot, col_slot, block.at[place], 0, start, rows, col, cols)
        up = pl.ds(start, rows)
        dst = out_ref.at[0, up, pl.ds(pl.multiple_of(owner * ROWS + col, TILE), cols)]
        copy = remote(f"gift{len(gifts)}", block.at[place, up, pl.ds(col, cols)], dst, peer)
        gifts.append(copy)
        return copy

    own_copy.wait()

    @pl.when(odd)
    def _():
        twin_own.wait_recv()
        tail_along.start()
        for h in range(2):
            across[h].wait_recv()

            @pl.when(has_next)
            def _(h=h):
                relay[h].start()

            along[h].wait_recv()
            far[h].start()

    @pl.when(even)
    def _():
        along[0].wait_recv()
        far[0].start()
        for h in range(2):
            across[h].wait_recv()
            twin_pair[h].start()

        @pl.when(has_prev)
        def _():
            tail_out.wait_recv()
            for h in range(2):
                relay[h].wait_recv()

        tail_along.start()
        round_one.start()
        along[1].wait_recv()
        far[1].start()

    split(OWN)
    keep(OWN, f)

    across[2].wait_recv()
    on(odd, twin_pair[0].wait_recv)
    split(PAIR, 0, HALF)
    tail_along.wait_recv()
    on(even, tail_far[0].start, tail_far[1].start, round_one.wait_recv, round_two.start)
    split(NEXT)
    make(0, PAIR, NEXT, f_next, pair, 0, HALF).start()

    @pl.when(even)
    def _():
        far[0].wait_recv()
        twin_far[0].start()

    keep(NEXT, f_next)
    near = make(2, NEXT, OWN, f, nxt)
    across[3].wait_recv()
    on(odd, twin_pair[1].wait_recv)
    split(PAIR, HALF, HALF)
    make(0, PAIR, NEXT, f_next, pair, HALF, HALF).start()

    far_gift = [None, None]

    def far_half(h):
        split(FAR, h * HALF, HALF)
        product(PAIR, FAR, block.at[1], 0, 0, ROWS, h * HALF, HALF)
        far_gift[h].start()

    for h in range(2):
        dst = out_ref.at[0, :, pl.ds(pl.multiple_of(f_far * ROWS + h * HALF, TILE), HALF)]
        far_gift[h] = remote(f"far_gift{h}", block.at[1, :, pl.ds(h * HALF, HALF)], dst, pair)
    gifts.extend(far_gift)

    @pl.when(odd)
    def _():
        far[0].wait_recv()
        twin_far[0].wait_recv()
        far_half(0)
        pl.semaphore_wait(go, 1)

    @pl.when(even)
    def _():
        far[1].wait_recv()
        twin_far[1].start()
        tail_far[0].wait_recv()
        pl.semaphore_signal(go, inc=1, device_id=twin, device_id_type=MESH)

    near.start()
    make(3, NEXT, PAIR, f_pair, nxt).start()

    @pl.when(even)
    def _():
        round_two.wait_recv()
        far_half(0)
        tail_far[1].wait_recv()

    @pl.when(odd)
    def _():
        far[1].wait_recv()
        twin_far[1].wait_recv()

    far_half(1)
    keep(PAIR, f_pair)
    keep(FAR, f_far)

    for copy in along + far + across + [tail_along]:
        copy.wait_send()
    on(has_next, tail_out.wait_send, label_out.wait_send, relay[0].wait_send, relay[1].wait_send)
    on(even, *(c.wait_send for c in [*tail_far, round_one, round_two, *twin_pair, *twin_far, twin_own, label_twin]))
    for copy in gifts:
        copy.wait()
    assert len(names) <= SEMAPHORES


SEMAPHORES = 32
AROUND = 128


def shards(intensity, cycle_label):
    rows, cols = intensity.shape
    return pl.pallas_call(
        kernel,
        out_shape=pltpu.VMEM((1, ROWS, 8 * ROWS), jnp.float32),
        in_specs=[pl.BlockSpec(memory_space=pltpu.HBM), pl.BlockSpec(memory_space=pltpu.HBM)],
        out_specs=pl.BlockSpec(memory_space=pltpu.VMEM),
        scratch_shapes=[
            pltpu.VMEM((4, ROWS, COLS), jnp.float32),
            pltpu.VMEM((4, ROWS, TAIL), jnp.float32),
            pltpu.VMEM((AROUND, TAIL), jnp.float32),
            pltpu.VMEM((1, COLS), jnp.int32),
            pltpu.VMEM((1, TAIL), jnp.int32),
            pltpu.VMEM((4, ROWS, DEPTH), jnp.bfloat16),
            pltpu.VMEM((4, ROWS, DEPTH), jnp.bfloat16),
            pltpu.VMEM((4, ROWS, 1), jnp.float32),
            pltpu.VMEM((4, 8, ROWS), jnp.float32),
            pltpu.VMEM((ROWS, 128), jnp.float32),
            pltpu.VMEM((4, ROWS, ROWS), jnp.float32),
            pltpu.SemaphoreType.DMA((SEMAPHORES,)),
            pltpu.SemaphoreType.DMA((SEMAPHORES,)),
            pltpu.SemaphoreType.DMA((2,)),
            pltpu.SemaphoreType.REGULAR,
        ],
        compiler_params=pltpu.CompilerParams(collective_id=0, has_side_effects=True, vmem_limit_bytes=55 << 20),
        name="gram_maps",
    )(intensity, cycle_label.reshape(1, cols))


def solution(mesh):
    in_specs = (P("frame", "pixel"), P("pixel"))
    out_specs = P("pixel", "frame", None)
    return jax.shard_map(shards, mesh=mesh, in_specs=in_specs, out_specs=out_specs, check_vma=False)
```

```python
import functools

import jax
import jax.numpy as jnp
from jax import lax
from jax.experimental import pallas as pl
from jax.experimental.pallas import tpu as pltpu
from jax.sharding import PartitionSpec as P

MESH = pl.DeviceIdType.MESH

OWN, NEXT, FAR, PAIR = range(4)
ROWS, COLS, TAIL = 512, 1024, 512
HALF = ROWS // 2
TILE = 256
DEPTH = COLS + TAIL

NT = (((1,), (1,)), ((), ()))


def kernel(
    x_ref, label_hbm, out_ref,
    xm, xt, passing, label_ref, tail_label, hi, lo, row_scale, col_scale, inverse, block, lifted, carried,
    send, recv, local, go,
):
    f = lax.axis_index("frame")
    r = lax.axis_index("pixel")
    a, b = f // 4, f % 4
    turn = 2 * (r % 2)
    f_next = a * 4 + (b + 1 + turn) % 4
    f_last = a * 4 + (b + 3 - turn) % 4
    f_far = a * 4 + (b + 2) % 4
    f_pair = (1 - a) * 4 + b
    f_carried = (1 - a) * 4 + (b + 3) % 4
    even = r % 2 == 0
    odd = r % 2 == 1
    has_next = jnp.logical_and(odd, r < 15)
    has_prev = jnp.logical_and(even, r > 0)
    nxt, last, pair = (f_next, r), (f_last, r), (f_pair, r)
    above = (a * 4 + (b + 1) % 4, r)
    twin = (f, r + 1 - turn)
    following = (f_pair, r + 1)
    preceding = (f_pair, r - 1)

    barrier = pltpu.get_barrier_semaphore()
    for peer in (nxt, last, pair, twin):
        pl.semaphore_signal(barrier, inc=1, device_id=peer, device_id_type=MESH)

    @pl.when(has_next)
    def _():
        pl.semaphore_signal(barrier, inc=1, device_id=following, device_id_type=MESH)

    @pl.when(has_prev)
    def _():
        pl.semaphore_signal(barrier, inc=1, device_id=preceding, device_id_type=MESH)

    crossing = jnp.logical_or(has_next, has_prev)

    @pl.when(crossing)
    def _():
        pl.semaphore_wait(barrier, 5)

    @pl.when(jnp.logical_not(crossing))
    def _():
        pl.semaphore_wait(barrier, 4)

    names = {}

    def remote(name, src, dst, peer):
        i = names.setdefault(name, len(names))
        return pltpu.make_async_remote_copy(src, dst, send.at[i], recv.at[i], device_id=peer, device_id_type=MESH)

    part = [pl.ds(0, HALF), pl.ds(HALF, HALF)]
    around = pl.ds(0, AROUND)
    rest = [pl.ds(AROUND, HALF - AROUND), pl.ds(HALF, HALF)]
    tail_cols = pl.ds(COLS - TAIL, TAIL)
    head_cols = pl.ds(0, COLS - TAIL)

    along = [remote(f"along{h}", x_ref.at[part[h]], xm.at[NEXT, part[h]], last) for h in range(2)]
    far = [remote(f"far{h}", xm.at[NEXT, part[h]], xm.at[FAR, part[h]], last) for h in range(2)]
    tail_along = remote("tail_along", xt.at[OWN], xt.at[NEXT], last)
    tail_far = [remote(f"tail_far{h}", xt.at[NEXT, p], xt.at[FAR, p], last) for h, p in enumerate(rest)]
    round_one = remote("round_one", xt.at[OWN, around], passing, nxt)
    round_two = remote("round_two", passing, xt.at[FAR, around], nxt)
    across = [
        remote(f"across{c}{h}", x_ref.at[part[h], cols], xm.at[PAIR, part[h], cols], pair)
        for c, cols in enumerate((tail_cols, head_cols))
        for h in range(2)
    ]
    tail_out = remote("tail_out", x_ref.at[:, tail_cols], xt.at[PAIR], following)
    relay = [
        remote(f"relay{h}", xm.at[PAIR, part[h], tail_cols], xt.at[OWN, part[h]], following) for h in range(2)
    ]
    label_out = remote("label_out", label_hbm.at[:, tail_cols], tail_label, following)
    label_twin = remote("label_twin", label_hbm.at[:, tail_cols], tail_label, twin)
    twin_own = remote("twin_own", x_ref.at[:, tail_cols], xt.at[OWN], twin)
    twin_pair, twin_far = (
        [remote(f"twin{s}{h}", xm.at[s, part[h], tail_cols], xt.at[s, part[h]], twin) for h in range(2)]
        for s in (PAIR, FAR)
    )

    def on(cond, *acts):
        @pl.when(cond)
        def _():
            for act in acts:
                act()

    own_copy = pltpu.make_async_copy(x_ref, xm.at[OWN], local.at[0])
    label_copy = pltpu.make_async_copy(label_hbm, label_ref, local.at[1])
    label_copy.start()
    on(has_next, tail_out.start, label_out.start)
    on(even, twin_own.start, label_twin.start)
    for h in range(4):
        across[h].start()
    for h in range(2):
        along[h].start()
    own_copy.start()

    @pl.when(has_prev)
    def _():
        label_out.wait_recv()

    on(odd, label_twin.wait_recv)
    label_copy.wait()

    @pl.when(r == 0)
    def _():
        xt[OWN] = jnp.zeros((ROWS, TAIL), jnp.float32)
        xt[PAIR] = jnp.zeros((ROWS, TAIL), jnp.float32)
        tail_label[...] = jnp.full((1, TAIL), -1, jnp.int32)

    keep_main = label_ref[...] == r
    keep_tail = tail_label[...] == r
    counts = jnp.sum(keep_main.astype(jnp.float32)) + jnp.sum(keep_tail.astype(jnp.float32))

    def split(slot, start=0, rows=ROWS, place=None):
        step = 64
        place = start if place is None else place

        def body(i, _):
            at = pl.ds(pl.multiple_of(start + i * step, step), step)
            to = pl.ds(pl.multiple_of(place + i * step, step), step)
            total = jnp.zeros((step, 1), jnp.float32)
            for ref, keep, base, width in ((xt, keep_tail, 0, TAIL), (xm, keep_main, TAIL, COLS)):
                v = jnp.where(keep, ref[slot, at, :], 0.0)
                v_hi = v.astype(jnp.bfloat16)
                v_lo = (v - v_hi.astype(jnp.float32)).astype(jnp.bfloat16)
                hi[slot, to, base : base + width] = v_hi
                lo[slot, to, base : base + width] = v_lo
                total = total + jnp.sum(v, axis=1, keepdims=True)
            row_scale[slot, to, :] = counts / total
            inverse[to, :] = jnp.broadcast_to(1.0 / total, (step, 128))
            return 0

        lax.fori_loop(0, rows // step, body, 0)
        for i in range(rows // 128):
            to = pl.ds(place + i * 128, 128)
            col_scale[slot, :, to] = inverse[to, :].T[0:8, :]

    def product(row_slot, col_slot, place, place_start, start=0, rows=ROWS, col=0, cols=ROWS):
        def body(i, _):
            at = pl.ds(pl.multiple_of(col + i * TILE, TILE), TILE)
            to = pl.ds(pl.multiple_of(place_start + col + i * TILE, TILE), TILE)
            up = pl.ds(start, rows)
            l_hi, l_lo = hi[row_slot, up, :], lo[row_slot, up, :]
            r_hi, r_lo = hi[col_slot, at, :], lo[col_slot, at, :]
            dot = functools.partial(lax.dot_general, dimension_numbers=NT, preferred_element_type=jnp.float32)
            total = dot(l_hi, r_hi) + (dot(l_hi, r_lo) + dot(l_lo, r_hi))
            place[up, to] = total * row_scale[row_slot, up, :] * col_scale[col_slot, 0:1, at]
            return 0

        lax.fori_loop(0, cols // TILE, body, 0)

    def keep(slot, owner):
        product(OWN, slot, out_ref.at[0], owner * ROWS)

    gifts = []

    def make(place, row_slot, col_slot, owner, peer, start=0, rows=ROWS, col=0, cols=ROWS):
        product(row_slot, col_slot, block.at[place], 0, start, rows, col, cols)
        up = pl.ds(start, rows)
        dst = out_ref.at[0, up, pl.ds(pl.multiple_of(owner * ROWS + col, TILE), cols)]
        copy = remote(f"gift{len(gifts)}", block.at[place, up, pl.ds(col, cols)], dst, peer)
        gifts.append(copy)
        return copy

    own_copy.wait()

    @pl.when(odd)
    def _():
        twin_own.wait_recv()
        tail_along.start()
        for h in range(2):
            across[h].wait_recv()

            @pl.when(has_next)
            def _(h=h):
                relay[h].start()

            along[h].wait_recv()
            far[h].start()

    @pl.when(even)
    def _():
        along[0].wait_recv()
        far[0].start()
        for h in range(2):
            across[h].wait_recv()
            twin_pair[h].start()

        @pl.when(has_prev)
        def _():
            tail_out.wait_recv()
            for h in range(2):
                relay[h].wait_recv()

        tail_along.start()
        round_one.start()
        along[1].wait_recv()
        far[1].start()

    split(OWN)
    keep(OWN, f)

    across[2].wait_recv()
    on(odd, twin_pair[0].wait_recv)
    split(PAIR, 0, HALF)
    tail_along.wait_recv()
    on(even, tail_far[0].start, tail_far[1].start, round_one.wait_recv, round_two.start)
    split(NEXT)
    make(0, PAIR, NEXT, f_next, pair, 0, HALF).start()

    @pl.when(even)
    def _():
        far[0].wait_recv()
        twin_far[0].start()

    keep(NEXT, f_next)
    near = make(2, NEXT, OWN, f, nxt)
    across[3].wait_recv()
    on(odd, twin_pair[1].wait_recv)
    split(PAIR, HALF, HALF)
    make(0, PAIR, NEXT, f_next, pair, HALF, HALF).start()

    far_gift = [None, None]
    below = pl.ds(LIFT, ROWS - LIFT)

    def far_half(h):
        split(FAR, h * HALF, HALF)
        product(PAIR, FAR, block.at[1], 0, LIFT, ROWS - LIFT, h * HALF, HALF)
        far_gift[h].start()

    for h in range(2):
        dst = out_ref.at[0, below, pl.ds(pl.multiple_of(f_far * ROWS + h * HALF, TILE), HALF)]
        far_gift[h] = remote(f"far_gift{h}", block.at[1, below, pl.ds(h * HALF, HALF)], dst, pair)
    gifts.extend(far_gift)

    lift = remote("lift", lifted, carried, above)
    dst = out_ref.at[0, pl.ds(0, LIFT), pl.ds(pl.multiple_of(f_carried * ROWS, ROWS), ROWS)]
    carry = remote("carry", carried, dst, above)
    gifts.append(carry)

    def start_lift():
        product(FAR, PAIR, lifted, 0, 0, LIFT)
        lift.start()

    @pl.when(odd)
    def _():
        far[0].wait_recv()
        twin_far[0].wait_recv()
        far_half(0)
        start_lift()
        pl.semaphore_wait(go, 1)

    @pl.when(even)
    def _():
        far[1].wait_recv()
        twin_far[1].start()
        tail_far[0].wait_recv()
        pl.semaphore_signal(go, inc=1, device_id=twin, device_id_type=MESH)

    near.start()

    @pl.when(even)
    def _():
        round_two.wait_recv()
        far_half(0)
        start_lift()

    make(3, NEXT, PAIR, f_pair, nxt, col=0, cols=HALF).start()
    second = make(3, NEXT, PAIR, f_pair, nxt, col=HALF, cols=HALF)
    on(odd, second.start)
    on(even, tail_far[1].wait_recv)

    @pl.when(odd)
    def _():
        far[1].wait_recv()
        twin_far[1].wait_recv()

    far_half(1)
    keep(PAIR, f_pair)
    lift.wait_recv()
    carry.start()
    on(even, second.start)
    keep(FAR, f_far)

    for copy in along + far + across + [tail_along, lift]:
        copy.wait_send()
    on(has_next, tail_out.wait_send, label_out.wait_send, relay[0].wait_send, relay[1].wait_send)
    on(even, *(c.wait_send for c in [*tail_far, round_one, round_two, *twin_pair, *twin_far, twin_own, label_twin]))
    for copy in gifts:
        copy.wait()
    assert len(names) <= SEMAPHORES


SEMAPHORES = 32
AROUND = 96
LIFT = 32


def shards(intensity, cycle_label):
    rows, cols = intensity.shape
    return pl.pallas_call(
        kernel,
        out_shape=pltpu.VMEM((1, ROWS, 8 * ROWS), jnp.float32),
        in_specs=[pl.BlockSpec(memory_space=pltpu.HBM), pl.BlockSpec(memory_space=pltpu.HBM)],
        out_specs=pl.BlockSpec(memory_space=pltpu.VMEM),
        scratch_shapes=[
            pltpu.VMEM((4, ROWS, COLS), jnp.float32),
            pltpu.VMEM((4, ROWS, TAIL), jnp.float32),
            pltpu.VMEM((AROUND, TAIL), jnp.float32),
            pltpu.VMEM((1, COLS), jnp.int32),
            pltpu.VMEM((1, TAIL), jnp.int32),
            pltpu.VMEM((4, ROWS, DEPTH), jnp.bfloat16),
            pltpu.VMEM((4, ROWS, DEPTH), jnp.bfloat16),
            pltpu.VMEM((4, ROWS, 1), jnp.float32),
            pltpu.VMEM((4, 8, ROWS), jnp.float32),
            pltpu.VMEM((ROWS, 128), jnp.float32),
            pltpu.VMEM((4, ROWS, ROWS), jnp.float32),
            pltpu.VMEM((LIFT, ROWS), jnp.float32),
            pltpu.VMEM((LIFT, ROWS), jnp.float32),
            pltpu.SemaphoreType.DMA((SEMAPHORES,)),
            pltpu.SemaphoreType.DMA((SEMAPHORES,)),
            pltpu.SemaphoreType.DMA((2,)),
            pltpu.SemaphoreType.REGULAR,
        ],
        compiler_params=pltpu.CompilerParams(collective_id=0, has_side_effects=True, vmem_limit_bytes=55 << 20),
        name="gram_maps",
    )(intensity, cycle_label.reshape(1, cols))


def solution(mesh):
    in_specs = (P("frame", "pixel"), P("pixel"))
    out_specs = P("pixel", "frame", None)
    return jax.shard_map(shards, mesh=mesh, in_specs=in_specs, out_specs=out_specs, check_vma=False)
```

```python
import functools

import jax
import jax.numpy as jnp
from jax import lax
from jax.experimental import pallas as pl
from jax.experimental.pallas import tpu as pltpu
from jax.sharding import PartitionSpec as P

MESH = pl.DeviceIdType.MESH

OWN, NEXT, FAR, PAIR = range(4)
ROWS, COLS, TAIL = 512, 1024, 512
HALF = ROWS // 2
TILE = 256
DEPTH = COLS + TAIL

NT = (((1,), (1,)), ((), ()))


def kernel(
    x_ref, label_hbm, out_ref,
    xm, xt, passing, label_ref, tail_label, hi, lo, row_scale, col_scale, inverse, block, lifted, carried,
    send, recv, local, go,
):
    f = lax.axis_index("frame")
    r = lax.axis_index("pixel")
    a, b = f // 4, f % 4
    turn = 2 * (r % 2)
    f_next = a * 4 + (b + 1 + turn) % 4
    f_last = a * 4 + (b + 3 - turn) % 4
    f_far = a * 4 + (b + 2) % 4
    f_pair = (1 - a) * 4 + b
    f_carried = (1 - a) * 4 + (b + 3) % 4
    even = r % 2 == 0
    odd = r % 2 == 1
    has_next = jnp.logical_and(odd, r < 15)
    has_prev = jnp.logical_and(even, r > 0)
    nxt, last, pair = (f_next, r), (f_last, r), (f_pair, r)
    above = (a * 4 + (b + 1) % 4, r)
    twin = (f, r + 1 - turn)
    following = (f_pair, r + 1)
    preceding = (f_pair, r - 1)

    barrier = pltpu.get_barrier_semaphore()
    for peer in (nxt, last, pair, twin):
        pl.semaphore_signal(barrier, inc=1, device_id=peer, device_id_type=MESH)

    @pl.when(has_next)
    def _():
        pl.semaphore_signal(barrier, inc=1, device_id=following, device_id_type=MESH)

    @pl.when(has_prev)
    def _():
        pl.semaphore_signal(barrier, inc=1, device_id=preceding, device_id_type=MESH)

    crossing = jnp.logical_or(has_next, has_prev)

    @pl.when(crossing)
    def _():
        pl.semaphore_wait(barrier, 5)

    @pl.when(jnp.logical_not(crossing))
    def _():
        pl.semaphore_wait(barrier, 4)

    names = {}

    def remote(name, src, dst, peer):
        i = names.setdefault(name, len(names))
        return pltpu.make_async_remote_copy(src, dst, send.at[i], recv.at[i], device_id=peer, device_id_type=MESH)

    part = [pl.ds(0, HALF), pl.ds(HALF, HALF)]
    around = pl.ds(0, AROUND)
    rest = [pl.ds(AROUND, HALF - AROUND), pl.ds(HALF, HALF)]
    tail_cols = pl.ds(COLS - TAIL, TAIL)
    head_cols = pl.ds(0, COLS - TAIL)

    along = [remote(f"along{h}", x_ref.at[part[h]], xm.at[NEXT, part[h]], last) for h in range(2)]
    far = [remote(f"far{h}", xm.at[NEXT, part[h]], xm.at[FAR, part[h]], last) for h in range(2)]
    tail_along = remote("tail_along", xt.at[OWN], xt.at[NEXT], last)
    tail_far = [remote(f"tail_far{h}", xt.at[NEXT, p], xt.at[FAR, p], last) for h, p in enumerate(rest)]
    round_one = remote("round_one", xt.at[OWN, around], passing, nxt)
    round_two = remote("round_two", passing, xt.at[FAR, around], nxt)
    across = [
        remote(f"across{c}{h}", x_ref.at[part[h], cols], xm.at[PAIR, part[h], cols], pair)
        for c, cols in enumerate((tail_cols, head_cols))
        for h in range(2)
    ]
    tail_out = remote("tail_out", x_ref.at[:, tail_cols], xt.at[PAIR], following)
    relay = [
        remote(f"relay{h}", xm.at[PAIR, part[h], tail_cols], xt.at[OWN, part[h]], following) for h in range(2)
    ]
    label_out = remote("label_out", label_hbm.at[:, tail_cols], tail_label, following)
    label_twin = remote("label_twin", label_hbm.at[:, tail_cols], tail_label, twin)
    twin_own = remote("twin_own", x_ref.at[:, tail_cols], xt.at[OWN], twin)
    twin_pair, twin_far = (
        [remote(f"twin{s}{h}", xm.at[s, part[h], tail_cols], xt.at[s, part[h]], twin) for h in range(2)]
        for s in (PAIR, FAR)
    )

    def on(cond, *acts):
        @pl.when(cond)
        def _():
            for act in acts:
                act()

    own_copy = pltpu.make_async_copy(x_ref, xm.at[OWN], local.at[0])
    label_copy = pltpu.make_async_copy(label_hbm, label_ref, local.at[1])
    label_copy.start()
    on(has_next, tail_out.start, label_out.start)
    on(even, twin_own.start, label_twin.start)
    for h in range(4):
        across[h].start()
    for h in range(2):
        along[h].start()
    own_copy.start()

    @pl.when(has_prev)
    def _():
        label_out.wait_recv()

    on(odd, label_twin.wait_recv)
    label_copy.wait()

    @pl.when(r == 0)
    def _():
        xt[OWN] = jnp.zeros((ROWS, TAIL), jnp.float32)
        xt[PAIR] = jnp.zeros((ROWS, TAIL), jnp.float32)
        tail_label[...] = jnp.full((1, TAIL), -1, jnp.int32)

    keep_main = label_ref[...] == r
    keep_tail = tail_label[...] == r
    counts = jnp.sum(keep_main.astype(jnp.float32)) + jnp.sum(keep_tail.astype(jnp.float32))

    def split(slot, start=0, rows=ROWS, place=None):
        step = 64
        place = start if place is None else place

        def body(i, _):
            at = pl.ds(pl.multiple_of(start + i * step, step), step)
            to = pl.ds(pl.multiple_of(place + i * step, step), step)
            total = jnp.zeros((step, 1), jnp.float32)
            for ref, keep, base, width in ((xt, keep_tail, 0, TAIL), (xm, keep_main, TAIL, COLS)):
                v = jnp.where(keep, ref[slot, at, :], 0.0)
                v_hi = v.astype(jnp.bfloat16)
                v_lo = (v - v_hi.astype(jnp.float32)).astype(jnp.bfloat16)
                hi[slot, to, base : base + width] = v_hi
                lo[slot, to, base : base + width] = v_lo
                total = total + jnp.sum(v, axis=1, keepdims=True)
            row_scale[slot, to, :] = counts / total
            inverse[to, :] = jnp.broadcast_to(1.0 / total, (step, 128))
            return 0

        lax.fori_loop(0, rows // step, body, 0)
        for i in range(rows // 128):
            to = pl.ds(place + i * 128, 128)
            col_scale[slot, :, to] = inverse[to, :].T[0:8, :]

    def product(row_slot, col_slot, place, place_start, start=0, rows=ROWS, col=0, cols=ROWS):
        def body(i, _):
            at = pl.ds(pl.multiple_of(col + i * TILE, TILE), TILE)
            to = pl.ds(pl.multiple_of(place_start + col + i * TILE, TILE), TILE)
            up = pl.ds(start, rows)
            l_hi, l_lo = hi[row_slot, up, :], lo[row_slot, up, :]
            r_hi, r_lo = hi[col_slot, at, :], lo[col_slot, at, :]
            dot = functools.partial(lax.dot_general, dimension_numbers=NT, preferred_element_type=jnp.float32)
            total = dot(l_hi, r_hi) + (dot(l_hi, r_lo) + dot(l_lo, r_hi))
            place[up, to] = total * row_scale[row_slot, up, :] * col_scale[col_slot, 0:1, at]
            return 0

        lax.fori_loop(0, cols // TILE, body, 0)

    def keep(slot, owner):
        product(OWN, slot, out_ref.at[0], owner * ROWS)

    gifts = []

    def make(place, row_slot, col_slot, owner, peer, start=0, rows=ROWS, col=0, cols=ROWS):
        product(row_slot, col_slot, block.at[place], 0, start, rows, col, cols)
        up = pl.ds(start, rows)
        dst = out_ref.at[0, up, pl.ds(pl.multiple_of(owner * ROWS + col, TILE), cols)]
        copy = remote(f"gift{len(gifts)}", block.at[place, up, pl.ds(col, cols)], dst, peer)
        gifts.append(copy)
        return copy

    own_copy.wait()

    @pl.when(odd)
    def _():
        twin_own.wait_recv()
        tail_along.start()
        for h in range(2):
            across[h].wait_recv()

            @pl.when(has_next)
            def _(h=h):
                relay[h].start()

            along[h].wait_recv()
            far[h].start()

    @pl.when(even)
    def _():
        along[0].wait_recv()
        far[0].start()
        for h in range(2):
            across[h].wait_recv()
            twin_pair[h].start()

        @pl.when(has_prev)
        def _():
            tail_out.wait_recv()
            for h in range(2):
                relay[h].wait_recv()

        tail_along.start()
        round_one.start()
        along[1].wait_recv()
        far[1].start()

    split(OWN)
    keep(OWN, f)

    across[2].wait_recv()
    on(odd, twin_pair[0].wait_recv)
    split(PAIR, 0, HALF)
    tail_along.wait_recv()
    on(even, tail_far[0].start, tail_far[1].start, round_one.wait_recv, round_two.start)
    split(NEXT)
    make(0, PAIR, NEXT, f_next, pair, 0, HALF).start()

    @pl.when(even)
    def _():
        far[0].wait_recv()
        twin_far[0].start()

    keep(NEXT, f_next)
    near = make(2, NEXT, OWN, f, nxt)
    across[3].wait_recv()
    on(odd, twin_pair[1].wait_recv)
    split(PAIR, HALF, HALF)
    make(0, PAIR, NEXT, f_next, pair, HALF, HALF).start()

    below = pl.ds(LIFT, ROWS - LIFT)

    def far_copy(h, up):
        dst = out_ref.at[0, up, pl.ds(pl.multiple_of(f_far * ROWS + h * HALF, TILE), HALF)]
        return remote(f"far_gift{h}", block.at[1, up, pl.ds(h * HALF, HALF)], dst, pair)

    whole = [far_copy(h, pl.ds(0, ROWS)) for h in range(2)]
    short = [far_copy(h, below) for h in range(2)]

    def far_half(h, start, copies):
        split(FAR, h * HALF, HALF)
        product(PAIR, FAR, block.at[1], 0, start, ROWS - start, h * HALF, HALF)
        copies[h].start()

    lift = remote("lift", lifted, carried, above)
    dst = out_ref.at[0, pl.ds(0, LIFT), pl.ds(pl.multiple_of(f_carried * ROWS, ROWS), ROWS)]
    carry = remote("carry", carried, dst, above)

    def start_lift():
        product(FAR, PAIR, lifted, 0, 0, LIFT)
        lift.start()

    @pl.when(odd)
    def _():
        far[0].wait_recv()
        twin_far[0].wait_recv()
        far_half(0, LIFT, short)
        start_lift()
        pl.semaphore_wait(go, 1)

    @pl.when(even)
    def _():
        far[1].wait_recv()
        twin_far[1].start()
        tail_far[0].wait_recv()
        pl.semaphore_signal(go, inc=1, device_id=twin, device_id_type=MESH)

    near.start()

    @pl.when(even)
    def _():
        round_two.wait_recv()
        far_half(0, 0, whole)

    make(3, NEXT, PAIR, f_pair, nxt, col=0, cols=HALF).start()
    second = make(3, NEXT, PAIR, f_pair, nxt, col=HALF, cols=HALF)
    second.start()

    @pl.when(even)
    def _():
        tail_far[1].wait_recv()
        far_half(1, 0, whole)

    @pl.when(odd)
    def _():
        far[1].wait_recv()
        twin_far[1].wait_recv()
        far_half(1, LIFT, short)
        lift.wait_recv()
        carry.start()

    keep(PAIR, f_pair)
    keep(FAR, f_far)

    for copy in along + far + across + [tail_along]:
        copy.wait_send()
    on(has_next, tail_out.wait_send, label_out.wait_send, relay[0].wait_send, relay[1].wait_send)
    on(even, *(c.wait_send for c in [*tail_far, round_one, round_two, *twin_pair, *twin_far, twin_own, label_twin]))
    on(odd, lift.wait_send, carry.wait, *(c.wait for c in short))
    on(even, *(c.wait for c in whole))
    for copy in gifts:
        copy.wait()
    assert len(names) <= SEMAPHORES


SEMAPHORES = 32
AROUND = 96
LIFT = 64


def shards(intensity, cycle_label):
    rows, cols = intensity.shape
    return pl.pallas_call(
        kernel,
        out_shape=pltpu.VMEM((1, ROWS, 8 * ROWS), jnp.float32),
        in_specs=[pl.BlockSpec(memory_space=pltpu.HBM), pl.BlockSpec(memory_space=pltpu.HBM)],
        out_specs=pl.BlockSpec(memory_space=pltpu.VMEM),
        scratch_shapes=[
            pltpu.VMEM((4, ROWS, COLS), jnp.float32),
            pltpu.VMEM((4, ROWS, TAIL), jnp.float32),
            pltpu.VMEM((AROUND, TAIL), jnp.float32),
            pltpu.VMEM((1, COLS), jnp.int32),
            pltpu.VMEM((1, TAIL), jnp.int32),
            pltpu.VMEM((4, ROWS, DEPTH), jnp.bfloat16),
            pltpu.VMEM((4, ROWS, DEPTH), jnp.bfloat16),
            pltpu.VMEM((4, ROWS, 1), jnp.float32),
            pltpu.VMEM((4, 8, ROWS), jnp.float32),
            pltpu.VMEM((ROWS, 128), jnp.float32),
            pltpu.VMEM((4, ROWS, ROWS), jnp.float32),
            pltpu.VMEM((LIFT, ROWS), jnp.float32),
            pltpu.VMEM((LIFT, ROWS), jnp.float32),
            pltpu.SemaphoreType.DMA((SEMAPHORES,)),
            pltpu.SemaphoreType.DMA((SEMAPHORES,)),
            pltpu.SemaphoreType.DMA((2,)),
            pltpu.SemaphoreType.REGULAR,
        ],
        compiler_params=pltpu.CompilerParams(collective_id=0, has_side_effects=True, vmem_limit_bytes=55 << 20),
        name="gram_maps",
    )(intensity, cycle_label.reshape(1, cols))


def solution(mesh):
    in_specs = (P("frame", "pixel"), P("pixel"))
    out_specs = P("pixel", "frame", None)
    return jax.shard_map(shards, mesh=mesh, in_specs=in_specs, out_specs=out_specs, check_vma=False)
```

```python
import functools

import jax
import jax.numpy as jnp
from jax import lax
from jax.experimental import pallas as pl
from jax.experimental.pallas import tpu as pltpu
from jax.sharding import PartitionSpec as P

MESH = pl.DeviceIdType.MESH

OWN, NEXT, FAR, PAIR = range(4)
ROWS, COLS, TAIL = 512, 1024, 512
HALF = ROWS // 2
TILE = 256
DEPTH = COLS + TAIL

NT = (((1,), (1,)), ((), ()))


def kernel(
    x_ref, label_hbm, out_ref,
    xm, xt, passing, label_ref, tail_label, hi, lo, row_scale, col_scale, inverse, block, lifted, carried,
    send, recv, local, go,
):
    f = lax.axis_index("frame")
    r = lax.axis_index("pixel")
    a, b = f // 4, f % 4
    turn = 2 * (r % 2)
    f_next = a * 4 + (b + 1 + turn) % 4
    f_last = a * 4 + (b + 3 - turn) % 4
    f_far = a * 4 + (b + 2) % 4
    f_pair = (1 - a) * 4 + b
    f_carried = (1 - a) * 4 + (b + 3) % 4
    even = r % 2 == 0
    odd = r % 2 == 1
    has_next = jnp.logical_and(odd, r < 15)
    has_prev = jnp.logical_and(even, r > 0)
    nxt, last, pair = (f_next, r), (f_last, r), (f_pair, r)
    above = (a * 4 + (b + 1) % 4, r)
    twin = (f, r + 1 - turn)
    following = (f_pair, r + 1)
    preceding = (f_pair, r - 1)

    barrier = pltpu.get_barrier_semaphore()
    for peer in (nxt, last, pair, twin):
        pl.semaphore_signal(barrier, inc=1, device_id=peer, device_id_type=MESH)

    @pl.when(has_next)
    def _():
        pl.semaphore_signal(barrier, inc=1, device_id=following, device_id_type=MESH)

    @pl.when(has_prev)
    def _():
        pl.semaphore_signal(barrier, inc=1, device_id=preceding, device_id_type=MESH)

    crossing = jnp.logical_or(has_next, has_prev)

    @pl.when(crossing)
    def _():
        pl.semaphore_wait(barrier, 5)

    @pl.when(jnp.logical_not(crossing))
    def _():
        pl.semaphore_wait(barrier, 4)

    names = {}

    def remote(name, src, dst, peer):
        i = names.setdefault(name, len(names))
        return pltpu.make_async_remote_copy(src, dst, send.at[i], recv.at[i], device_id=peer, device_id_type=MESH)

    part = [pl.ds(0, HALF), pl.ds(HALF, HALF)]
    around = pl.ds(0, AROUND)
    rest = [pl.ds(AROUND, HALF - AROUND), pl.ds(HALF, HALF)]
    tail_cols = pl.ds(COLS - TAIL, TAIL)
    head_cols = pl.ds(0, COLS - TAIL)

    along = [remote(f"along{h}", x_ref.at[part[h]], xm.at[NEXT, part[h]], last) for h in range(2)]
    far = [remote(f"far{h}", xm.at[NEXT, part[h]], xm.at[FAR, part[h]], last) for h in range(2)]
    tail_along = remote("tail_along", xt.at[OWN], xt.at[NEXT], last)
    tail_far = [remote(f"tail_far{h}", xt.at[NEXT, p], xt.at[FAR, p], last) for h, p in enumerate(rest)]
    round_one = remote("round_one", xt.at[OWN, around], passing, nxt)
    round_two = remote("round_two", passing, xt.at[FAR, around], nxt)
    across = [
        remote(f"across{c}{h}", x_ref.at[part[h], cols], xm.at[PAIR, part[h], cols], pair)
        for c, cols in enumerate((tail_cols, head_cols))
        for h in range(2)
    ]
    tail_out = remote("tail_out", x_ref.at[:, tail_cols], xt.at[PAIR], following)
    relay = [
        remote(f"relay{h}", xm.at[PAIR, part[h], tail_cols], xt.at[OWN, part[h]], following) for h in range(2)
    ]
    label_out = remote("label_out", label_hbm.at[:, tail_cols], tail_label, following)
    label_twin = remote("label_twin", label_hbm.at[:, tail_cols], tail_label, twin)
    twin_own = remote("twin_own", x_ref.at[:, tail_cols], xt.at[OWN], twin)
    twin_pair, twin_far = (
        [remote(f"twin{s}{h}", xm.at[s, part[h], tail_cols], xt.at[s, part[h]], twin) for h in range(2)]
        for s in (PAIR, FAR)
    )

    def on(cond, *acts):
        @pl.when(cond)
        def _():
            for act in acts:
                act()

    own_copy = pltpu.make_async_copy(x_ref, xm.at[OWN], local.at[0])
    label_copy = pltpu.make_async_copy(label_hbm, label_ref, local.at[1])
    label_copy.start()
    on(has_next, tail_out.start, label_out.start)
    on(even, twin_own.start, label_twin.start)
    for h in range(4):
        across[h].start()
    for h in range(2):
        along[h].start()
    own_copy.start()

    @pl.when(has_prev)
    def _():
        label_out.wait_recv()

    on(odd, label_twin.wait_recv)
    label_copy.wait()

    @pl.when(r == 0)
    def _():
        xt[OWN] = jnp.zeros((ROWS, TAIL), jnp.float32)
        xt[PAIR] = jnp.zeros((ROWS, TAIL), jnp.float32)
        tail_label[...] = jnp.full((1, TAIL), -1, jnp.int32)

    keep_main = label_ref[...] == r
    keep_tail = tail_label[...] == r
    counts = jnp.sum(keep_main.astype(jnp.float32)) + jnp.sum(keep_tail.astype(jnp.float32))

    def split(slot, start=0, rows=ROWS, place=None):
        step = 64
        place = start if place is None else place

        def body(i, _):
            at = pl.ds(pl.multiple_of(start + i * step, step), step)
            to = pl.ds(pl.multiple_of(place + i * step, step), step)
            total = jnp.zeros((step, 1), jnp.float32)
            for ref, keep, base, width in ((xt, keep_tail, 0, TAIL), (xm, keep_main, TAIL, COLS)):
                v = jnp.where(keep, ref[slot, at, :], 0.0)
                v_hi = v.astype(jnp.bfloat16)
                v_lo = (v - v_hi.astype(jnp.float32)).astype(jnp.bfloat16)
                hi[slot, to, base : base + width] = v_hi
                lo[slot, to, base : base + width] = v_lo
                total = total + jnp.sum(v, axis=1, keepdims=True)
            row_scale[slot, to, :] = counts / total
            inverse[to, :] = jnp.broadcast_to(1.0 / total, (step, 128))
            return 0

        lax.fori_loop(0, rows // step, body, 0)
        for i in range(rows // 128):
            to = pl.ds(place + i * 128, 128)
            col_scale[slot, :, to] = inverse[to, :].T[0:8, :]

    def product(row_slot, col_slot, place, place_start, start=0, rows=ROWS, col=0, cols=ROWS):
        def body(i, _):
            at = pl.ds(pl.multiple_of(col + i * TILE, TILE), TILE)
            to = pl.ds(pl.multiple_of(place_start + col + i * TILE, TILE), TILE)
            up = pl.ds(start, rows)
            l_hi, l_lo = hi[row_slot, up, :], lo[row_slot, up, :]
            r_hi, r_lo = hi[col_slot, at, :], lo[col_slot, at, :]
            dot = functools.partial(lax.dot_general, dimension_numbers=NT, preferred_element_type=jnp.float32)
            total = dot(l_hi, r_hi) + (dot(l_hi, r_lo) + dot(l_lo, r_hi))
            place[up, to] = total * row_scale[row_slot, up, :] * col_scale[col_slot, 0:1, at]
            return 0

        lax.fori_loop(0, cols // TILE, body, 0)

    def keep(slot, owner):
        product(OWN, slot, out_ref.at[0], owner * ROWS)

    gifts = []

    def make(place, row_slot, col_slot, owner, peer, start=0, rows=ROWS, col=0, cols=ROWS):
        product(row_slot, col_slot, block.at[place], 0, start, rows, col, cols)
        up = pl.ds(start, rows)
        dst = out_ref.at[0, up, pl.ds(pl.multiple_of(owner * ROWS + col, TILE), cols)]
        copy = remote(f"gift{len(gifts)}", block.at[place, up, pl.ds(col, cols)], dst, peer)
        gifts.append(copy)
        return copy

    own_copy.wait()

    @pl.when(odd)
    def _():
        twin_own.wait_recv()
        tail_along.start()
        for h in range(2):
            across[h].wait_recv()

            @pl.when(has_next)
            def _(h=h):
                relay[h].start()

            along[h].wait_recv()
            far[h].start()

    @pl.when(even)
    def _():
        along[0].wait_recv()
        far[0].start()
        for h in range(2):
            across[h].wait_recv()
            twin_pair[h].start()

        @pl.when(has_prev)
        def _():
            tail_out.wait_recv()
            for h in range(2):
                relay[h].wait_recv()

        tail_along.start()
        round_one.start()
        along[1].wait_recv()
        far[1].start()

    split(OWN)
    keep(OWN, f)

    across[2].wait_recv()
    on(odd, twin_pair[0].wait_recv)
    split(PAIR, 0, HALF)
    tail_along.wait_recv()
    on(even, tail_far[0].start, tail_far[1].start, round_one.wait_recv, round_two.start)
    split(NEXT)
    make(0, PAIR, NEXT, f_next, pair, 0, HALF).start()

    @pl.when(even)
    def _():
        far[0].wait_recv()
        twin_far[0].start()

    keep(NEXT, f_next)
    near = make(2, NEXT, OWN, f, nxt)
    across[3].wait_recv()
    on(odd, twin_pair[1].wait_recv)
    split(PAIR, HALF, HALF)
    make(0, PAIR, NEXT, f_next, pair, HALF, HALF).start()

    below = pl.ds(LIFT, ROWS - LIFT)

    def far_copy(h, up):
        dst = out_ref.at[0, up, pl.ds(pl.multiple_of(f_far * ROWS + h * HALF, TILE), HALF)]
        return remote(f"far_gift{h}", block.at[1, up, pl.ds(h * HALF, HALF)], dst, pair)

    whole = [far_copy(h, pl.ds(0, ROWS)) for h in range(2)]
    short = [far_copy(h, below) for h in range(2)]

    def far_half(h, start, copies):
        split(FAR, h * HALF, HALF)
        product(PAIR, FAR, block.at[1], 0, start, ROWS - start, h * HALF, HALF)
        copies[h].start()

    lift = remote("lift", lifted, carried, above)
    dst = out_ref.at[0, pl.ds(0, LIFT), pl.ds(pl.multiple_of(f_carried * ROWS, ROWS), ROWS)]
    carry = remote("carry", carried, dst, above)

    def start_lift():
        product(FAR, PAIR, lifted, 0, 0, LIFT)
        lift.start()

    @pl.when(odd)
    def _():
        far[0].wait_recv()
        twin_far[0].wait_recv()
        far_half(0, LIFT, short)
        start_lift()
        pl.semaphore_wait(go, 1)

    @pl.when(even)
    def _():
        far[1].wait_recv()
        twin_far[1].start()
        tail_far[0].wait_recv()
        pl.semaphore_signal(go, inc=1, device_id=twin, device_id_type=MESH)

    near.start()

    @pl.when(even)
    def _():
        round_two.wait_recv()
        far_half(0, 0, whole)

    make(3, NEXT, PAIR, f_pair, nxt, col=0, cols=HALF).start()
    second = make(3, NEXT, PAIR, f_pair, nxt, col=HALF, cols=HALF)
    second.start()

    @pl.when(even)
    def _():
        tail_far[1].wait_recv()
        far_half(1, 0, whole)

    @pl.when(odd)
    def _():
        far[1].wait_recv()
        twin_far[1].wait_recv()
        far_half(1, LIFT, short)
        lift.wait_recv()
        carry.start()

    keep(PAIR, f_pair)
    keep(FAR, f_far)

    for copy in along + far + across + [tail_along]:
        copy.wait_send()
    on(has_next, tail_out.wait_send, label_out.wait_send, relay[0].wait_send, relay[1].wait_send)
    on(even, *(c.wait_send for c in [*tail_far, round_one, round_two, *twin_pair, *twin_far, twin_own, label_twin]))
    on(odd, lift.wait_send, carry.wait, *(c.wait for c in short))
    on(even, *(c.wait for c in whole))
    for copy in gifts:
        copy.wait()
    assert len(names) <= SEMAPHORES


SEMAPHORES = 32
AROUND = 112
LIFT = 64


def shards(intensity, cycle_label):
    rows, cols = intensity.shape
    return pl.pallas_call(
        kernel,
        out_shape=pltpu.VMEM((1, ROWS, 8 * ROWS), jnp.float32),
        in_specs=[pl.BlockSpec(memory_space=pltpu.HBM), pl.BlockSpec(memory_space=pltpu.HBM)],
        out_specs=pl.BlockSpec(memory_space=pltpu.VMEM),
        scratch_shapes=[
            pltpu.VMEM((4, ROWS, COLS), jnp.float32),
            pltpu.VMEM((4, ROWS, TAIL), jnp.float32),
            pltpu.VMEM((AROUND, TAIL), jnp.float32),
            pltpu.VMEM((1, COLS), jnp.int32),
            pltpu.VMEM((1, TAIL), jnp.int32),
            pltpu.VMEM((4, ROWS, DEPTH), jnp.bfloat16),
            pltpu.VMEM((4, ROWS, DEPTH), jnp.bfloat16),
            pltpu.VMEM((4, ROWS, 1), jnp.float32),
            pltpu.VMEM((4, 8, ROWS), jnp.float32),
            pltpu.VMEM((ROWS, 128), jnp.float32),
            pltpu.VMEM((4, ROWS, ROWS), jnp.float32),
            pltpu.VMEM((LIFT, ROWS), jnp.float32),
            pltpu.VMEM((LIFT, ROWS), jnp.float32),
            pltpu.SemaphoreType.DMA((SEMAPHORES,)),
            pltpu.SemaphoreType.DMA((SEMAPHORES,)),
            pltpu.SemaphoreType.DMA((2,)),
            pltpu.SemaphoreType.REGULAR,
        ],
        compiler_params=pltpu.CompilerParams(collective_id=0, has_side_effects=True, vmem_limit_bytes=55 << 20),
        name="gram_maps",
    )(intensity, cycle_label.reshape(1, cols))


def solution(mesh):
    in_specs = (P("frame", "pixel"), P("pixel"))
    out_specs = P("pixel", "frame", None)
    return jax.shard_map(shards, mesh=mesh, in_specs=in_specs, out_specs=out_specs, check_vma=False)
```
